256 devices in a mesh: frame: 16 (over y, z_hi, core), patch: 16 (over x, z_lo).
Axes of the slice: x: 4, y: 4, z: 8 (z_hi: 2, z_lo: 4; z = z_hi * 4 + z_lo), core: 2. Of those that a mesh axis runs over, the one named last changes fastest.
Arguments:
- q_space: bfloat16 [128, 8, 1024, 128], P('frame', None, 'patch'), may hold values from -8 to 8
- k_space: bfloat16 [128, 8, 1024, 128], P('frame', None, 'patch'), may hold values from -8 to 8
- v_space: bfloat16 [128, 8, 1024, 128], P('frame', None, 'patch'), may hold values from -6 to 6
- d_out_space: bfloat16 [128, 8, 1024, 128], P('frame', None, 'patch'), may hold values from -6 to 6
- q_time: bfloat16 [128, 8, 1024, 128], P('frame', None, 'patch'), may hold values from -8 to 8
- k_time: bfloat16 [128, 8, 1024, 128], P('frame', None, 'patch'), may hold values from -8 to 8
- v_time: bfloat16 [128, 8, 1024, 128], P('frame', None, 'patch'), may hold values from -6 to 6
- d_out_time: bfloat16 [128, 8, 1024, 128], P('frame', None, 'patch'), may hold values from -6 to 6
Outputs:
- grad_q_space: bfloat16 [128, 8, 1024, 128], P('frame', None, 'patch')
- grad_k_space: bfloat16 [128, 8, 1024, 128], P('frame', None, 'patch')
- grad_v_space: bfloat16 [128, 8, 1024, 128], P('frame', None, 'patch')
- grad_q_time: bfloat16 [128, 8, 1024, 128], P('frame', None, 'patch')
- grad_k_time: bfloat16 [128, 8, 1024, 128], P('frame', None, 'patch')
- grad_v_time: bfloat16 [128, 8, 1024, 128], P('frame', None, 'patch')
The draws below stay inside these ranges and needn't reach their ends.
All inputs are finite; a program needn't handle non-finite values.
Results may differ from the reference program's by a relative error of at most 0.0071.
Values may be sent and summed in bfloat16 or wider, within the bound.
No kernel may reach another device: no remote copies, remote signals or barrier semaphores. Data moves between devices by JAX's collectives and lax.ppermute only.
A program may use at most 128 MiB of HBM per device.

```python
import math
import jax
import jax.numpy as jnp
from jax import lax

HEADS = 8
HEAD_DIM = 128
FRAMES = 128
PATCHES = 1024


def pair_draw(key, salt_value, item_shape, length, width):
    key = jax.random.fold_in(key, salt_value)
    subkeys = jax.random.split(key, 3)
    full_shape = item_shape + (length, width)
    query_rows = jnp.clip(jax.random.normal(subkeys[0], full_shape, jnp.float32), -6.0, 6.0)
    key_rows = jnp.clip(jax.random.normal(subkeys[2], full_shape, jnp.float32), -6.0, 6.0)
    return (query_rows, key_rows)


def draw_q_space(key, part):
    return pair_draw(key, 11, (FRAMES, HEADS), PATCHES, HEAD_DIM)[0].astype(jnp.bfloat16)


def draw_k_space(key, part):
    return pair_draw(key, 11, (FRAMES, HEADS), PATCHES, HEAD_DIM)[1].astype(jnp.bfloat16)


def draw_q_time(key, part):
    return jnp.transpose(pair_draw(key, 23, (HEADS, PATCHES), FRAMES, HEAD_DIM)[0], (2, 0, 1, 3)).astype(jnp.bfloat16)


def draw_k_time(key, part):
    return jnp.transpose(pair_draw(key, 23, (HEADS, PATCHES), FRAMES, HEAD_DIM)[1], (2, 0, 1, 3)).astype(jnp.bfloat16)


def steps_of(rng, extent, pieces, least, high):
    def one(dim, shards_of):
        heights = jax.random.uniform(jax.random.fold_in(jax.random.fold_in(rng, 6), dim), (shards_of,), jnp.float32, least / len(pieces), high / len(pieces))
        return jnp.repeat(jnp.exp(heights), extent[dim] // shards_of).reshape((-1,) + (1,) * (len(extent) - dim - 1))

    level = one(*pieces[0])
    for cut in pieces[1:]:
        level = level * one(*cut)
    return level


def scatter_about(stream_key, shape, deviation, reach, cuts=(), kind=jnp.bfloat16):
    loudness = steps_of(stream_key, shape, cuts, -0.22, 0.18) if cuts else 1.0
    values = jax.random.normal(stream_key, shape, jnp.float32) * deviation * loudness
    return jnp.minimum(jnp.maximum(values, -reach), reach).astype(kind)


def setup_inputs(seed: int = 0) -> dict:
    splits = jax.random.split(jax.random.key(seed), 9)
    return {
        "q_space": draw_q_space(jax.random.fold_in(splits[8], 71), 0),
        "k_space": draw_k_space(jax.random.fold_in(splits[8], 71), 0),
        "v_space": scatter_about(splits[2], (FRAMES, HEADS, PATCHES, HEAD_DIM), 1.0, 6.0, ((0, 16), (2, 16))),
        "d_out_space": scatter_about(splits[3], (FRAMES, HEADS, PATCHES, HEAD_DIM), 1.0, 6.0, ((0, 16), (2, 16))),
        "q_time": draw_q_time(jax.random.fold_in(splits[8], 71), 0),
        "k_time": draw_k_time(jax.random.fold_in(splits[8], 71), 0),
        "v_time": scatter_about(splits[6], (FRAMES, HEADS, PATCHES, HEAD_DIM), 1.0, 6.0, ((0, 16), (2, 16))),
        "d_out_time": scatter_about(splits[7], (FRAMES, HEADS, PATCHES, HEAD_DIM), 1.0, 6.0, ((0, 16), (2, 16))),
    }


def attention_grads(queries, key_rows, values, out_grad, causal):
    inverse_root_scale = 1.0 / math.sqrt(queries.shape[-1])
    query_wide = queries.astype(jnp.float32)
    key_wide = key_rows.astype(jnp.float32)
    value_wide = values.astype(jnp.float32)
    gradient_upstream = out_grad.astype(jnp.float32)
    score_logits = jnp.einsum('uej,uoj->ueo', query_wide, key_wide) * inverse_root_scale
    if causal:
        length = score_logits.shape[-1]
        allowed = jnp.arange(length)[:, None] >= jnp.arange(length)[None, :]
        score_logits = jnp.where(allowed, score_logits, -1e+30)
    row_max = lax.optimization_barrier(jnp.max(score_logits, axis=-1, keepdims=True))
    raised = jnp.exp(score_logits - row_max)
    softmax_rows = raised / lax.optimization_barrier(jnp.sum(raised, axis=-1, keepdims=True))
    weight_probabilities = lax.optimization_barrier(softmax_rows.astype(jnp.bfloat16)).astype(jnp.float32)
    output_tensor = jnp.einsum('jgf,jfi->jgi', weight_probabilities, value_wide)
    delta_rows = lax.optimization_barrier(jnp.sum(gradient_upstream * output_tensor, axis=-1))
    value_gradient = jnp.einsum('euw,euh->ewh', weight_probabilities, gradient_upstream).astype(jnp.bfloat16)
    probability_gradient = jnp.einsum('uej,uoj->ueo', gradient_upstream, value_wide)
    logit_gradient = softmax_rows * (probability_gradient - delta_rows[..., None])
    logit_gradient = lax.optimization_barrier(logit_gradient.astype(jnp.bfloat16)).astype(jnp.float32)
    query_gradient = (jnp.einsum('jgf,jfi->jgi', logit_gradient, key_wide) * inverse_root_scale).astype(jnp.bfloat16)
    key_gradient = (jnp.einsum('euw,euh->ewh', logit_gradient, query_wide) * inverse_root_scale).astype(jnp.bfloat16)
    return (query_gradient, key_gradient, value_gradient)

def space_frame(parts):
    return attention_grads(parts[0], parts[1], parts[2], parts[3], False)

def time_head(parts):
    return attention_grads(parts[0], parts[1], parts[2], parts[3], True)

def reference(q_space, k_space, v_space, d_out_space, q_time, k_time, v_time, d_out_time):
    space_q, space_k, space_v = lax.map(space_frame, (q_space, k_space, v_space, d_out_space))
    moved = tuple((jnp.transpose(block, (1, 2, 0, 3)) for block in (q_time, k_time, v_time, d_out_time)))
    time_q, time_k, time_v = lax.map(time_head, moved)
    time_q = jnp.transpose(time_q, (2, 0, 1, 3))
    time_k = jnp.transpose(time_k, (2, 0, 1, 3))
    time_v = jnp.transpose(time_v, (2, 0, 1, 3))
    return (space_q, space_k, space_v, time_q, time_k, time_v)
```

```python
import functools
import math

import jax
import jax.numpy as jnp
from jax import lax
from jax.experimental import pallas as pl
from jax.experimental.pallas import tpu as pltpu
from jax.sharding import PartitionSpec as P

F32 = jnp.float32
BF16 = jnp.bfloat16
LOG2E = 1.4426950408889634
MASKED = -1e30
VMEM_LIMIT = 40 * 1024 * 1024

CORE_BIT = 1
ZHI_BIT = 2
Y_BIT = 4
FRAME_DEVICES = 16
PATCH_DEVICES = 16
CHUNKS = 2


def dot(a, b, dims):
    return lax.dot_general(a, b, (dims, ((), ())), preferred_element_type=F32)


NT = ((1,), (1,))
NN = ((1,), (0,))
TN = ((0,), (0,))


def space_kernel(x_ref, o_ref, dk_acc, dv_acc, *, block, scale):
    peers, _, _, rows, dim = x_ref.shape
    length = peers * rows
    k = x_ref[:, 0, 1].reshape(length, dim)
    v = x_ref[:, 0, 2].reshape(length, dim)
    per = block // rows
    for b in range(length // block):
        q = x_ref[b * per : (b + 1) * per, 0, 0].reshape(block, dim)
        g = x_ref[b * per : (b + 1) * per, 0, 3].reshape(block, dim)
        s = dot(k, q, NT) * (scale * LOG2E)
        top = jnp.max(s, axis=0, keepdims=True)
        e = jnp.exp2(s - top)
        p = e * (1.0 / jnp.sum(e, axis=0, keepdims=True))
        w = p.astype(BF16)
        gv = dot(v, g, NT)
        delta = jnp.sum(p * gv, axis=0, keepdims=True)
        ds = (p * (gv - delta)).astype(BF16)
        dv = dot(w, g, NN)
        dk = dot(ds, q, NN)
        if b == 0:
            dv_acc[...] = dv
            dk_acc[...] = dk
        else:
            dv_acc[...] += dv
            dk_acc[...] += dk
        dq = dot(ds, k, TN) * scale
        o_ref[b * per : (b + 1) * per, 0, 0] = dq.astype(BF16).reshape(per, rows, dim)
    o_ref[:, 0, 1] = (dk_acc[...] * scale).astype(BF16).reshape(peers, rows, dim)
    o_ref[:, 0, 2] = dv_acc[...].astype(BF16).reshape(peers, rows, dim)


def space_grads(x):
    peers, seqs, _, rows, dim = x.shape
    length = peers * rows
    flops = seqs * 5 * 2 * length * length * dim
    return pl.pallas_call(
        functools.partial(space_kernel, block=256, scale=1.0 / math.sqrt(dim)),
        grid=(seqs,),
        in_specs=[pl.BlockSpec((peers, 1, 4, rows, dim), lambda j: (0, j, 0, 0, 0))],
        out_specs=pl.BlockSpec((peers, 1, 3, rows, dim), lambda j: (0, j, 0, 0, 0)),
        out_shape=jax.ShapeDtypeStruct((peers, seqs, 3, rows, dim), BF16),
        scratch_shapes=[pltpu.VMEM((length, dim), F32), pltpu.VMEM((length, dim), F32)],
        cost_estimate=pl.CostEstimate(
            flops=flops, bytes_accessed=x.size * 2 * 2, transcendentals=seqs * length * length
        ),
        compiler_params=pltpu.CompilerParams(vmem_limit_bytes=VMEM_LIMIT),
        name="space_grads",
    )(x)


def frame_rows(side, count, rows, dim_of):
    i = lax.broadcasted_iota(jnp.int32, *dim_of)
    return (2 * (i // rows) + side) * rows + i % rows


def time_scores(side, qg_ref, rb_ref, ra_ref, kv_ref, p, scale):
    slots, _, _, rows, dim = qg_ref.shape
    half = slots * rows
    k = kv_ref[:, 0, p].reshape(half, dim)
    v = kv_ref[:, 1, p].reshape(half, dim)
    q = jnp.concatenate(
        [qg_ref[:, 0, p].reshape(half, dim), rb_ref[0, p], ra_ref[:, 0, p].reshape(half - rows, dim)]
    )
    g = jnp.concatenate(
        [qg_ref[:, 1, p].reshape(half, dim), rb_ref[1, p], ra_ref[:, 1, p].reshape(half - rows, dim)]
    )
    s = dot(k, q, NT) * (scale * LOG2E)
    gv = dot(v, g, NT)
    return q, g, k, s, gv


def time_allowed(side, slots, rows):
    half = slots * rows
    shape = (half, 2 * half)
    ki = lax.broadcasted_iota(jnp.int32, shape, 0)
    qi = lax.broadcasted_iota(jnp.int32, shape, 1)
    remote = qi // half
    qj = qi % half
    key_frame = (2 * (ki // rows) + side) * rows + ki % rows
    query_side = jnp.where(remote == 0, side, 1 - side)
    query_frame = (2 * (qj // rows) + query_side) * rows + qj % rows
    return key_frame <= query_frame


def time_stats_kernel(side_ref, qg_ref, rb_ref, ra_ref, kv_ref, st_ref, *, scale):
    slots, _, count, rows, _ = qg_ref.shape
    side = side_ref[0]
    allowed = time_allowed(side, slots, rows)
    for p in range(count):
        _, _, _, s, gv = time_scores(side, qg_ref, rb_ref, ra_ref, kv_ref, p, scale)
        s = jnp.where(allowed, s, MASKED)
        top = jnp.max(s, axis=0, keepdims=True)
        e = jnp.exp2(s - top)
        total = jnp.sum(e, axis=0, keepdims=True)
        st_ref[0, pl.ds(p, 1)] = top + jnp.log2(total)
        st_ref[1, pl.ds(p, 1)] = jnp.sum(e * gv, axis=0, keepdims=True) / total


def time_grads_kernel(
    side_ref, qg_ref, rb_ref, ra_ref, kv_ref, mine_ref, other_ref, dq_ref, db_ref, da_ref, dkv_ref, *, scale
):
    slots, _, count, rows, dim = qg_ref.shape
    half = slots * rows
    side = side_ref[0]
    allowed = time_allowed(side, slots, rows)
    lse_a, lse_b = mine_ref[0], other_ref[0]
    top = jnp.maximum(lse_a, lse_b)
    lse = top + jnp.log2(jnp.exp2(lse_a - top) + jnp.exp2(lse_b - top))
    delta = jnp.exp2(lse_a - lse) * mine_ref[1] + jnp.exp2(lse_b - lse) * other_ref[1]
    for p in range(count):
        q, g, k, s, gv = time_scores(side, qg_ref, rb_ref, ra_ref, kv_ref, p, scale)
        w = jnp.where(allowed, jnp.exp2(jnp.where(allowed, s - lse[p : p + 1], 0.0)), 0.0)
        ds = (w * (gv - delta[p : p + 1])).astype(BF16)
        w = w.astype(BF16)
        dkv_ref[:, 1, p] = dot(w, g, NN).astype(BF16).reshape(slots, rows, dim)
        dkv_ref[:, 0, p] = (dot(ds, q, NN) * scale).astype(BF16).reshape(slots, rows, dim)
        dq = dot(ds, k, TN) * scale
        dq_ref[:, p] = dq[:half].reshape(slots, rows, dim)
        db_ref[p] = dq[half : half + rows].astype(BF16)
        da_ref[:, p] = dq[half + rows :].astype(BF16).reshape(slots - 1, rows, dim)


def time_specs(group, slots, rows, dim):
    return [
        pl.BlockSpec(memory_space=pltpu.SMEM),
        pl.BlockSpec((slots, 2, group, rows, dim), lambda i: (0, 0, i, 0, 0)),
        pl.BlockSpec((2, group, rows, dim), lambda i: (0, i, 0, 0)),
        pl.BlockSpec((slots - 1, 2, group, rows, dim), lambda i: (0, 0, i, 0, 0)),
        pl.BlockSpec((slots, 2, group, rows, dim), lambda i: (0, 0, i, 0, 0)),
    ]


def time_stats(side, qg, rb, ra, kv, group=8):
    slots, _, count, rows, dim = qg.shape
    half = slots * rows
    return pl.pallas_call(
        functools.partial(time_stats_kernel, scale=1.0 / math.sqrt(dim)),
        grid=(count // group,),
        in_specs=time_specs(group, slots, rows, dim),
        out_specs=pl.BlockSpec((2, group, 2 * half), lambda i: (0, i, 0)),
        out_shape=jax.ShapeDtypeStruct((2, count, 2 * half), F32),
        cost_estimate=pl.CostEstimate(
            flops=count * 2 * 2 * half * 2 * half * dim,
            bytes_accessed=qg.size * 2 * 3,
            transcendentals=count * half * 2 * half,
        ),
        compiler_params=pltpu.CompilerParams(vmem_limit_bytes=VMEM_LIMIT),
        name="time_stats",
    )(side, qg, rb, ra, kv)


def time_grads(side, qg, rb, ra, kv, mine, other, group=8):
    slots, _, count, rows, dim = qg.shape
    half = slots * rows
    stat = pl.BlockSpec((2, group, 2 * half), lambda i: (0, i, 0))
    return pl.pallas_call(
        functools.partial(time_grads_kernel, scale=1.0 / math.sqrt(dim)),
        grid=(count // group,),
        in_specs=time_specs(group, slots, rows, dim) + [stat, stat],
        out_specs=[
            pl.BlockSpec((slots, group, rows, dim), lambda i: (0, i, 0, 0)),
            pl.BlockSpec((group, rows, dim), lambda i: (i, 0, 0)),
            pl.BlockSpec((slots - 1, group, rows, dim), lambda i: (0, i, 0, 0)),
            pl.BlockSpec((slots, 2, group, rows, dim), lambda i: (0, 0, i, 0, 0)),
        ],
        out_shape=[
            jax.ShapeDtypeStruct((slots, count, rows, dim), F32),
            jax.ShapeDtypeStruct((count, rows, dim), BF16),
            jax.ShapeDtypeStruct((slots - 1, count, rows, dim), BF16),
            jax.ShapeDtypeStruct((slots, 2, count, rows, dim), BF16),
        ],
        cost_estimate=pl.CostEstimate(
            flops=count * 5 * 2 * half * 2 * half * dim,
            bytes_accessed=qg.size * 2 * 5,
            transcendentals=count * half * 2 * half,
        ),
        compiler_params=pltpu.CompilerParams(vmem_limit_bytes=VMEM_LIMIT),
        name="time_grads",
    )(side, qg, rb, ra, kv, mine, other)


def swap(x, bits):
    return lax.ppermute(x, "frame", [(i, i ^ bits) for i in range(FRAME_DEVICES)])


def from_side(x, side):
    pairs = [(i, i ^ ZHI_BIT) for i in range(FRAME_DEVICES) if (i // ZHI_BIT) % 2 == side]
    return lax.ppermute(x, "frame", pairs)


def pick(x, i):
    return lax.dynamic_index_in_dim(x, i, 0, keepdims=False)


def y_exchange(u, y):
    got = [swap(pick(u, y ^ j), j * Y_BIT) for j in range(1, 4)]
    for j in range(1, 4):
        u = lax.dynamic_update_index_in_dim(u, got[j - 1], y ^ j, 0)
    return u


def gather_frames(arrays, y, core):
    t = jnp.stack([jnp.transpose(a, (1, 2, 0, 3)) for a in arrays], 1)
    t = t.reshape((2, t.shape[0] // 2) + t.shape[1:])
    keep, got = pick(t, core), swap(pick(t, 1 - core), CORE_BIT)
    first = core == 0
    u = jnp.concatenate([jnp.where(first, keep, got), jnp.where(first, got, keep)], axis=-2)
    return y_exchange(u, y)


def scatter_frames(u, y, core):
    v = y_exchange(u, y)
    half = v.shape[-2] // 2
    low, high = v[..., :half, :], v[..., half:, :]
    first = core == 0
    keep = jnp.where(first, low, high)
    got = swap(jnp.where(first, high, low), CORE_BIT)
    t = jnp.concatenate([jnp.where(first, keep, got), jnp.where(first, got, keep)], axis=0)
    return [jnp.transpose(t[:, i], (2, 0, 1, 3)) for i in range(t.shape[1])]


def exchange_patches(x):
    return lax.all_to_all(x, "patch", split_axis=0, concat_axis=0, tiled=True)


def per_device(q_space, k_space, v_space, d_out_space, q_time, k_time, v_time, d_out_time):
    frames, heads, rows, dim = q_space.shape
    seqs = frames * heads
    f = lax.axis_index("frame")
    y, side, core = f // Y_BIT, (f // ZHI_BIT) % 2, f % 2
    side_arr = jnp.reshape(side, (1,)).astype(jnp.int32)

    space = [a.reshape(seqs, rows, dim) for a in (q_space, k_space, v_space, d_out_space)]
    width = seqs // CHUNKS
    arrived = []
    for c in range(CHUNKS):
        x = jnp.stack([a[c * width : (c + 1) * width] for a in space], 1)
        arrived.append(exchange_patches(x.reshape(PATCH_DEVICES, width // PATCH_DEVICES, 4, rows, dim)))

    qg = gather_frames((q_time, d_out_time), y, core)
    ra = swap(qg[1:], ZHI_BIT)
    rb = from_side(qg[0], 1)
    kv = gather_frames((k_time, v_time), y, core)

    back = [exchange_patches(space_grads(x)).reshape(width, 3, rows, dim) for x in arrived]

    mine = time_stats(side_arr, qg, rb, ra, kv)
    other = swap(mine, ZHI_BIT)
    other = jnp.roll(other, other.shape[-1] // 2, axis=-1)
    dq, db, da, dkv = time_grads(side_arr, qg, rb, ra, kv, mine, other)
    da = swap(da, ZHI_BIT)
    db = from_side(db, 0)
    dq = (dq + jnp.concatenate([db[None], da]).astype(F32)).astype(BF16)
    dk_time, dv_time = scatter_frames(dkv, y, core)
    (dq_time,) = scatter_frames(dq[:, None], y, core)

    shape = (frames, heads, rows, dim)
    out = [jnp.concatenate([b[:, i] for b in back]).reshape(shape) for i in range(3)]
    return (out[0], out[1], out[2], dq_time, dk_time, dv_time)


def solution(mesh):
    spec = P("frame", None, "patch", None)
    return jax.shard_map(
        per_device, mesh=mesh, in_specs=(spec,) * 8, out_specs=(spec,) * 6, check_vma=False
    )
```

```python
import functools
import math

import jax
import jax.numpy as jnp
from jax import lax
from jax.experimental import pallas as pl
from jax.experimental.pallas import tpu as pltpu
from jax.sharding import PartitionSpec as P

F32 = jnp.float32
BF16 = jnp.bfloat16
LOG2E = 1.4426950408889634
MASKED = -1e30
VMEM_LIMIT = 40 * 1024 * 1024

CORE_BIT = 1
ZHI_BIT = 2
Y_BIT = 4
FRAME_DEVICES = 16
PATCH_DEVICES = 16
CHUNKS = 2


def dot(a, b, dims):
    return lax.dot_general(a, b, (dims, ((), ())), preferred_element_type=F32)


NT = ((1,), (1,))
NN = ((1,), (0,))
TN = ((0,), (0,))


def space_kernel(x_ref, o_ref, dk_acc, dv_acc, *, block, scale):
    peers, _, _, rows, dim = x_ref.shape
    length = peers * rows
    k = x_ref[:, 0, 1].reshape(length, dim)
    v = x_ref[:, 0, 2].reshape(length, dim)
    per = block // rows
    for b in range(length // block):
        q = x_ref[b * per : (b + 1) * per, 0, 0].reshape(block, dim)
        g = x_ref[b * per : (b + 1) * per, 0, 3].reshape(block, dim)
        s = dot(k, q, NT) * (scale * LOG2E)
        top = jnp.max(s, axis=0, keepdims=True)
        e = jnp.exp2(s - top)
        p = e * (1.0 / jnp.sum(e, axis=0, keepdims=True))
        w = p.astype(BF16)
        gv = dot(v, g, NT)
        delta = jnp.sum(p * gv, axis=0, keepdims=True)
        ds = (p * (gv - delta)).astype(BF16)
        dv = dot(w, g, NN)
        dk = dot(ds, q, NN)
        if b == 0:
            dv_acc[...] = dv
            dk_acc[...] = dk
        else:
            dv_acc[...] += dv
            dk_acc[...] += dk
        dq = dot(ds, k, TN) * scale
        o_ref[b * per : (b + 1) * per, 0, 0] = dq.astype(BF16).reshape(per, rows, dim)
    o_ref[:, 0, 1] = (dk_acc[...] * scale).astype(BF16).reshape(peers, rows, dim)
    o_ref[:, 0, 2] = dv_acc[...].astype(BF16).reshape(peers, rows, dim)


def space_grads(x):
    peers, seqs, _, rows, dim = x.shape
    length = peers * rows
    flops = seqs * 5 * 2 * length * length * dim
    return pl.pallas_call(
        functools.partial(space_kernel, block=256, scale=1.0 / math.sqrt(dim)),
        grid=(seqs,),
        in_specs=[pl.BlockSpec((peers, 1, 4, rows, dim), lambda j: (0, j, 0, 0, 0))],
        out_specs=pl.BlockSpec((peers, 1, 3, rows, dim), lambda j: (0, j, 0, 0, 0)),
        out_shape=jax.ShapeDtypeStruct((peers, seqs, 3, rows, dim), BF16),
        scratch_shapes=[pltpu.VMEM((length, dim), F32), pltpu.VMEM((length, dim), F32)],
        cost_estimate=pl.CostEstimate(
            flops=flops, bytes_accessed=x.size * 2 * 2, transcendentals=seqs * length * length
        ),
        compiler_params=pltpu.CompilerParams(vmem_limit_bytes=VMEM_LIMIT),
        name="space_grads",
    )(x)


def time_rows(qg_ref, rb_ref, ra_ref, part, p):
    slots, _, _, rows, dim = qg_ref.shape
    half = slots * rows
    return jnp.concatenate(
        [
            qg_ref[:, part, p].reshape(half, dim),
            rb_ref[part, p],
            ra_ref[:, part, p].reshape(half - rows, dim),
        ]
    )


def time_allowed(side, slots, rows):
    half = slots * rows
    shape = (half, 2 * half)
    ki = lax.broadcasted_iota(jnp.int32, shape, 0)
    qi = lax.broadcasted_iota(jnp.int32, shape, 1)
    remote = qi // half
    qj = qi % half
    key_frame = (2 * (ki // rows) + side) * rows + ki % rows
    query_side = jnp.where(remote == 0, side, 1 - side)
    query_frame = (2 * (qj // rows) + query_side) * rows + qj % rows
    return key_frame <= query_frame


def time_stats_kernel(side_ref, qg_ref, rb_ref, ra_ref, kv_ref, st_ref, *, scale):
    slots, _, count, rows, _ = qg_ref.shape
    side = side_ref[0]
    half = slots * rows
    allowed = time_allowed(side, slots, rows)
    patches = range(count)
    dim = qg_ref.shape[-1]
    s = [dot(kv_ref[:, 0, p].reshape(half, dim), time_rows(qg_ref, rb_ref, ra_ref, 0, p), NT) for p in patches]
    gv = [dot(kv_ref[:, 1, p].reshape(half, dim), time_rows(qg_ref, rb_ref, ra_ref, 1, p), NT) for p in patches]
    s = [jnp.where(allowed, x * (scale * LOG2E), MASKED) for x in s]
    top = [jnp.max(x, axis=0, keepdims=True) for x in s]
    e = [jnp.exp2(x - t) for x, t in zip(s, top)]
    total = [jnp.sum(x, axis=0, keepdims=True) for x in e]
    part = [jnp.sum(x * y, axis=0, keepdims=True) for x, y in zip(e, gv)]
    st_ref[0] = jnp.concatenate([t + jnp.log2(x) for t, x in zip(top, total)])
    st_ref[1] = jnp.concatenate([x / y for x, y in zip(part, total)])


def time_totals(mine_ref, other_ref):
    lse_a, lse_b = mine_ref[0], other_ref[0]
    top = jnp.maximum(lse_a, lse_b)
    lse = top + jnp.log2(jnp.exp2(lse_a - top) + jnp.exp2(lse_b - top))
    delta = jnp.exp2(lse_a - lse) * mine_ref[1] + jnp.exp2(lse_b - lse) * other_ref[1]
    return lse, delta


def time_weights(allowed, s, gv, lse, delta):
    w = jnp.where(allowed, jnp.exp2(jnp.where(allowed, s - lse, 0.0)), 0.0)
    return w, (w * (gv - delta)).astype(BF16)


def time_grads_kernel(
    side_ref, qg_ref, rb_ref, ra_ref, kv_ref, mine_ref, other_ref, dq_ref, db_ref, da_ref, dkv_ref, *, scale
):
    slots, _, count, rows, dim = qg_ref.shape
    half = slots * rows
    allowed = time_allowed(side_ref[0], slots, rows)
    lse, delta = time_totals(mine_ref, other_ref)
    patches = range(count)
    k = [kv_ref[:, 0, p].reshape(half, dim) for p in patches]
    q = [time_rows(qg_ref, rb_ref, ra_ref, 0, p) for p in patches]
    g = [time_rows(qg_ref, rb_ref, ra_ref, 1, p) for p in patches]
    s = [dot(k[p], q[p], NT) * (scale * LOG2E) for p in patches]
    gv = [dot(kv_ref[:, 1, p].reshape(half, dim), g[p], NT) for p in patches]
    both = [time_weights(allowed, s[p], gv[p], lse[p : p + 1], delta[p : p + 1]) for p in patches]
    dv = [dot(both[p][0].astype(BF16), g[p], NN) for p in patches]
    dk = [dot(both[p][1], q[p], NN) for p in patches]
    dq = [dot(both[p][1], k[p], TN) for p in patches]
    for p in patches:
        dkv_ref[:, 1, p] = dv[p].astype(BF16).reshape(slots, rows, dim)
        dkv_ref[:, 0, p] = (dk[p] * scale).astype(BF16).reshape(slots, rows, dim)
        x = dq[p] * scale
        dq_ref[:, p] = x[:half].reshape(slots, rows, dim)
        db_ref[p] = x[half : half + rows].astype(BF16)
        da_ref[:, p] = x[half + rows :].astype(BF16).reshape(slots - 1, rows, dim)


def time_specs(group, slots, rows, dim):
    return [
        pl.BlockSpec(memory_space=pltpu.SMEM),
        pl.BlockSpec((slots, 2, group, rows, dim), lambda i: (0, 0, i, 0, 0)),
        pl.BlockSpec((2, group, rows, dim), lambda i: (0, i, 0, 0)),
        pl.BlockSpec((slots - 1, 2, group, rows, dim), lambda i: (0, 0, i, 0, 0)),
        pl.BlockSpec((slots, 2, group, rows, dim), lambda i: (0, 0, i, 0, 0)),
    ]


def time_stats(side, qg, rb, ra, kv, group=8):
    slots, _, count, rows, dim = qg.shape
    half = slots * rows
    return pl.pallas_call(
        functools.partial(time_stats_kernel, scale=1.0 / math.sqrt(dim)),
        grid=(count // group,),
        in_specs=time_specs(group, slots, rows, dim),
        out_specs=pl.BlockSpec((2, group, 2 * half), lambda i: (0, i, 0)),
        out_shape=jax.ShapeDtypeStruct((2, count, 2 * half), F32),
        cost_estimate=pl.CostEstimate(
            flops=count * 2 * 2 * half * 2 * half * dim,
            bytes_accessed=qg.size * 2 * 3,
            transcendentals=count * half * 2 * half,
        ),
        compiler_params=pltpu.CompilerParams(vmem_limit_bytes=VMEM_LIMIT),
        name="time_stats",
    )(side, qg, rb, ra, kv)


def time_grads(side, qg, rb, ra, kv, mine, other, group=8):
    slots, _, count, rows, dim = qg.shape
    half = slots * rows
    stat = pl.BlockSpec((2, group, 2 * half), lambda i: (0, i, 0))
    return pl.pallas_call(
        functools.partial(time_grads_kernel, scale=1.0 / math.sqrt(dim)),
        grid=(count // group,),
        in_specs=time_specs(group, slots, rows, dim) + [stat, stat],
        out_specs=[
            pl.BlockSpec((slots, group, rows, dim), lambda i: (0, i, 0, 0)),
            pl.BlockSpec((group, rows, dim), lambda i: (i, 0, 0)),
            pl.BlockSpec((slots - 1, group, rows, dim), lambda i: (0, i, 0, 0)),
            pl.BlockSpec((slots, 2, group, rows, dim), lambda i: (0, 0, i, 0, 0)),
        ],
        out_shape=[
            jax.ShapeDtypeStruct((slots, count, rows, dim), F32),
            jax.ShapeDtypeStruct((count, rows, dim), BF16),
            jax.ShapeDtypeStruct((slots - 1, count, rows, dim), BF16),
            jax.ShapeDtypeStruct((slots, 2, count, rows, dim), BF16),
        ],
        cost_estimate=pl.CostEstimate(
            flops=count * 5 * 2 * half * 2 * half * dim,
            bytes_accessed=qg.size * 2 * 5,
            transcendentals=count * half * 2 * half,
        ),
        compiler_params=pltpu.CompilerParams(vmem_limit_bytes=VMEM_LIMIT),
        name="time_grads",
    )(side, qg, rb, ra, kv, mine, other)


def swap(x, bits):
    return lax.ppermute(x, "frame", [(i, i ^ bits) for i in range(FRAME_DEVICES)])


def from_side(x, side):
    pairs = [(i, i ^ ZHI_BIT) for i in range(FRAME_DEVICES) if (i // ZHI_BIT) % 2 == side]
    return lax.ppermute(x, "frame", pairs)


def pick(x, i):
    return lax.dynamic_index_in_dim(x, i, 0, keepdims=False)


def y_exchange(u, y):
    got = [swap(pick(u, y ^ j), j * Y_BIT) for j in range(1, 4)]
    for j in range(1, 4):
        u = lax.dynamic_update_index_in_dim(u, got[j - 1], y ^ j, 0)
    return u


def gather_frames(arrays, y, core):
    t = jnp.stack([jnp.transpose(a, (1, 2, 0, 3)) for a in arrays], 1)
    t = t.reshape((2, t.shape[0] // 2) + t.shape[1:])
    keep, got = pick(t, core), swap(pick(t, 1 - core), CORE_BIT)
    first = core == 0
    u = jnp.concatenate([jnp.where(first, keep, got), jnp.where(first, got, keep)], axis=-2)
    return y_exchange(u, y)


def scatter_frames(u, y, core):
    slots, n, count, rows, dim = u.shape
    t = jnp.transpose(u.reshape(slots, n, count, 2, rows // 2, dim), (0, 3, 1, 4, 2, 5))
    out = [jnp.zeros((rows // 2, 2 * slots, count, dim), u.dtype) for _ in range(n)]
    for j in range(slots):
        for c in range(2):
            piece = pick(pick(t, y ^ j), core ^ c)
            if j or c:
                piece = swap(piece, j * Y_BIT + c * CORE_BIT)
            head = (core ^ c) * slots + (y ^ j)
            out = [lax.dynamic_update_index_in_dim(o, piece[i], head, 1) for i, o in enumerate(out)]
    return out


def exchange_patches(x):
    return lax.all_to_all(x, "patch", split_axis=0, concat_axis=0, tiled=True)


def after(values, done):
    return lax.optimization_barrier(tuple(values) + (done,))


def per_device(q_space, k_space, v_space, d_out_space, q_time, k_time, v_time, d_out_time):
    frames, heads, rows, dim = q_space.shape
    seqs = frames * heads
    f = lax.axis_index("frame")
    y, side, core = f // Y_BIT, (f // ZHI_BIT) % 2, f % 2
    side_arr = jnp.reshape(side, (1,)).astype(jnp.int32)

    space = [a.reshape(seqs, rows, dim) for a in (q_space, k_space, v_space, d_out_space)]
    width = seqs // CHUNKS

    def space_part(c):
        x = jnp.stack([a[c * width : (c + 1) * width] for a in space], 1)
        return x.reshape(PATCH_DEVICES, width // PATCH_DEVICES, 4, rows, dim)

    first, second = space_part(0), space_part(1)
    first = exchange_patches(first)
    qg = gather_frames((q_time, d_out_time), y, core)
    ra = swap(qg[1:], ZHI_BIT)
    rb = from_side(qg[0], 1)
    k_time, v_time, first, second, qg = after((k_time, v_time, first, second), qg)
    second = exchange_patches(second)
    kv = gather_frames((k_time, v_time), y, core)
    first = space_grads(first)

    kv, rb, first, second = lax.optimization_barrier((kv, rb, first, second))
    first, _ = after((first,), ra)
    first = exchange_patches(first)
    mine = time_stats(side_arr, qg, rb, ra, kv)
    other = swap(mine, ZHI_BIT)
    other = jnp.roll(other, other.shape[-1] // 2, axis=-1)
    second = space_grads(second)
    second, other = after((second,), other)
    dq, db, da, dkv = time_grads(side_arr, qg, rb, ra, kv, mine, other)
    db_sent, da_sent = from_side(db, 0), swap(da, ZHI_BIT)
    second, _ = after((second,), da)
    second = exchange_patches(second)
    dkv, first = after((dkv,), first)
    dk_time, dv_time = scatter_frames(dkv, y, core)
    dq, dk_time = after((dq,), dk_time)
    dq = (dq + jnp.concatenate([db_sent[None], da_sent]).astype(F32)).astype(BF16)
    (dq_time,) = scatter_frames(dq[:, None], y, core)
    second, dq_time = after((second,), dq_time)
    back = [x.reshape(width, 3, rows, dim) for x in (first, second)]

    shape = (frames, heads, rows, dim)
    out = [jnp.concatenate([b[:, i] for b in back]).reshape(shape) for i in range(3)]
    return (out[0], out[1], out[2], dq_time, dk_time, dv_time)


def solution(mesh):
    spec = P("frame", None, "patch", None)
    return jax.shard_map(
        per_device, mesh=mesh, in_specs=(spec,) * 8, out_specs=(spec,) * 6, check_vma=False
    )
```

```python
import functools
import math

import jax
import jax.numpy as jnp
from jax import lax
from jax.experimental import pallas as pl
from jax.experimental.pallas import tpu as pltpu
from jax.sharding import PartitionSpec as P

F32 = jnp.float32
BF16 = jnp.bfloat16
LOG2E = 1.4426950408889634
MASKED = -1e30
VMEM_LIMIT = 40 * 1024 * 1024

CORE_BIT = 1
ZHI_BIT = 2
Y_BIT = 4
FRAME_DEVICES = 16
PATCH_DEVICES = 16
CHUNKS = 2


def dot(a, b, dims):
    return lax.dot_general(a, b, (dims, ((), ())), preferred_element_type=F32)


NT = ((1,), (1,))
NN = ((1,), (0,))
TN = ((0,), (0,))


def space_kernel(x_ref, o_ref, dk_acc, dv_acc, *, block, scale):
    peers, _, _, rows, dim = x_ref.shape
    length = peers * rows
    k = x_ref[:, 0, 1].reshape(length, dim)
    v = x_ref[:, 0, 2].reshape(length, dim)
    per = block // rows
    for b in range(length // block):
        q = x_ref[b * per : (b + 1) * per, 0, 0].reshape(block, dim)
        g = x_ref[b * per : (b + 1) * per, 0, 3].reshape(block, dim)
        s = dot(k, q, NT) * (scale * LOG2E)
        top = jnp.max(s, axis=0, keepdims=True)
        e = jnp.exp2(s - top)
        p = e * (1.0 / jnp.sum(e, axis=0, keepdims=True))
        w = p.astype(BF16)
        gv = dot(v, g, NT)
        delta = jnp.sum(p * gv, axis=0, keepdims=True)
        ds = (p * (gv - delta)).astype(BF16)
        dv = dot(w, g, NN)
        dk = dot(ds, q, NN)
        if b == 0:
            dv_acc[...] = dv
            dk_acc[...] = dk
        else:
            dv_acc[...] += dv
            dk_acc[...] += dk
        dq = dot(ds, k, TN) * scale
        o_ref[b * per : (b + 1) * per, 0, 0] = dq.astype(BF16).reshape(per, rows, dim)
    o_ref[:, 0, 1] = (dk_acc[...] * scale).astype(BF16).reshape(peers, rows, dim)
    o_ref[:, 0, 2] = dv_acc[...].astype(BF16).reshape(peers, rows, dim)


def space_grads(x):
    peers, seqs, _, rows, dim = x.shape
    length = peers * rows
    flops = seqs * 5 * 2 * length * length * dim
    return pl.pallas_call(
        functools.partial(space_kernel, block=256, scale=1.0 / math.sqrt(dim)),
        grid=(seqs,),
        in_specs=[pl.BlockSpec((peers, 1, 4, rows, dim), lambda j: (0, j, 0, 0, 0))],
        out_specs=pl.BlockSpec((peers, 1, 3, rows, dim), lambda j: (0, j, 0, 0, 0)),
        out_shape=jax.ShapeDtypeStruct((peers, seqs, 3, rows, dim), BF16),
        scratch_shapes=[pltpu.VMEM((length, dim), F32), pltpu.VMEM((length, dim), F32)],
        cost_estimate=pl.CostEstimate(
            flops=flops, bytes_accessed=x.size * 2 * 2, transcendentals=seqs * length * length
        ),
        compiler_params=pltpu.CompilerParams(vmem_limit_bytes=VMEM_LIMIT),
        name="space_grads",
    )(x)


def stack_kernel(q_ref, k_ref, v_ref, g_ref, o_ref):
    for i, x in enumerate((q_ref, k_ref, v_ref, g_ref)):
        o_ref[:, i] = x[...]


def stack_seqs(arrays, start, count, group=16):
    _, rows, dim = arrays[0].shape
    return pl.pallas_call(
        stack_kernel,
        grid=(count // group,),
        in_specs=[pl.BlockSpec((group, rows, dim), lambda i: (i + start // group, 0, 0))] * 4,
        out_specs=pl.BlockSpec((group, 4, rows, dim), lambda i: (i, 0, 0, 0)),
        out_shape=jax.ShapeDtypeStruct((count, 4, rows, dim), BF16),
        cost_estimate=pl.CostEstimate(flops=0, bytes_accessed=count * rows * dim * 16, transcendentals=0),
        name="stack_seqs",
    )(*arrays)


def unstack_kernel(x_ref, *refs):
    for i, o in enumerate(refs[-3:]):
        o[...] = x_ref[:, i]


def unstack_seqs(x, start, total, into=(), group=16):
    count, _, rows, dim = x.shape
    return pl.pallas_call(
        unstack_kernel,
        grid=(count // group,),
        in_specs=[pl.BlockSpec((group, 3, rows, dim), lambda i: (i, 0, 0, 0))]
        + [pl.BlockSpec(memory_space=pl.ANY)] * len(into),
        out_specs=[pl.BlockSpec((group, rows, dim), lambda i: (i + start // group, 0, 0))] * 3,
        out_shape=[jax.ShapeDtypeStruct((total, rows, dim), BF16)] * 3,
        input_output_aliases={i + 1: i for i in range(len(into))},
        cost_estimate=pl.CostEstimate(flops=0, bytes_accessed=count * rows * dim * 12, transcendentals=0),
        name="unstack_seqs",
    )(x, *into)


def time_rows(qg_ref, rb_ref, ra_ref, part, p):
    slots, _, _, rows, dim = qg_ref.shape
    half = slots * rows
    return jnp.concatenate(
        [
            qg_ref[:, part, p].reshape(half, dim),
            rb_ref[part, p],
            ra_ref[:, part, p].reshape(half - rows, dim),
        ]
    )


def time_allowed(side, slots, rows):
    half = slots * rows
    shape = (half, 2 * half)
    ki = lax.broadcasted_iota(jnp.int32, shape, 0)
    qi = lax.broadcasted_iota(jnp.int32, shape, 1)
    remote = qi // half
    qj = qi % half
    key_frame = (2 * (ki // rows) + side) * rows + ki % rows
    query_side = jnp.where(remote == 0, side, 1 - side)
    query_frame = (2 * (qj // rows) + query_side) * rows + qj % rows
    return key_frame <= query_frame


def time_stats_kernel(side_ref, qg_ref, rb_ref, ra_ref, kv_ref, st_ref, *, scale):
    slots, _, count, rows, _ = qg_ref.shape
    side = side_ref[0]
    half = slots * rows
    allowed = time_allowed(side, slots, rows)
    patches = range(count)
    dim = qg_ref.shape[-1]
    s = [dot(kv_ref[:, 0, p].reshape(half, dim), time_rows(qg_ref, rb_ref, ra_ref, 0, p), NT) for p in patches]
    gv = [dot(kv_ref[:, 1, p].reshape(half, dim), time_rows(qg_ref, rb_ref, ra_ref, 1, p), NT) for p in patches]
    s = [jnp.where(allowed, x * (scale * LOG2E), MASKED) for x in s]
    top = [jnp.max(x, axis=0, keepdims=True) for x in s]
    e = [jnp.exp2(x - t) for x, t in zip(s, top)]
    total = [jnp.sum(x, axis=0, keepdims=True) for x in e]
    part = [jnp.sum(x * y, axis=0, keepdims=True) for x, y in zip(e, gv)]
    st_ref[0] = jnp.concatenate([t + jnp.log2(x) for t, x in zip(top, total)])
    st_ref[1] = jnp.concatenate([x / y for x, y in zip(part, total)])


def time_totals(mine_ref, other_ref):
    lse_a, lse_b = mine_ref[0], other_ref[0]
    top = jnp.maximum(lse_a, lse_b)
    lse = top + jnp.log2(jnp.exp2(lse_a - top) + jnp.exp2(lse_b - top))
    delta = jnp.exp2(lse_a - lse) * mine_ref[1] + jnp.exp2(lse_b - lse) * other_ref[1]
    return lse, delta


def time_weights(allowed, s, gv, lse, delta):
    w = jnp.where(allowed, jnp.exp2(jnp.where(allowed, s - lse, 0.0)), 0.0)
    return w, (w * (gv - delta)).astype(BF16)


def time_grads_kernel(
    side_ref, qg_ref, rb_ref, ra_ref, kv_ref, mine_ref, other_ref, dq_ref, db_ref, da_ref, dkv_ref, *, scale
):
    slots, _, count, rows, dim = qg_ref.shape
    half = slots * rows
    allowed = time_allowed(side_ref[0], slots, rows)
    lse, delta = time_totals(mine_ref, other_ref)
    patches = range(count)
    k = [kv_ref[:, 0, p].reshape(half, dim) for p in patches]
    q = [time_rows(qg_ref, rb_ref, ra_ref, 0, p) for p in patches]
    g = [time_rows(qg_ref, rb_ref, ra_ref, 1, p) for p in patches]
    s = [dot(k[p], q[p], NT) * (scale * LOG2E) for p in patches]
    gv = [dot(kv_ref[:, 1, p].reshape(half, dim), g[p], NT) for p in patches]
    both = [time_weights(allowed, s[p], gv[p], lse[p : p + 1], delta[p : p + 1]) for p in patches]
    dv = [dot(both[p][0].astype(BF16), g[p], NN) for p in patches]
    dk = [dot(both[p][1], q[p], NN) for p in patches]
    dq = [dot(both[p][1], k[p], TN) for p in patches]
    for p in patches:
        dkv_ref[:, 1, p] = dv[p].astype(BF16).reshape(slots, rows, dim)
        dkv_ref[:, 0, p] = (dk[p] * scale).astype(BF16).reshape(slots, rows, dim)
        x = dq[p] * scale
        dq_ref[:, p] = x[:half].reshape(slots, rows, dim)
        db_ref[p] = x[half : half + rows].astype(BF16)
        da_ref[:, p] = x[half + rows :].astype(BF16).reshape(slots - 1, rows, dim)


def time_specs(group, slots, rows, dim):
    return [
        pl.BlockSpec(memory_space=pltpu.SMEM),
        pl.BlockSpec((slots, 2, group, rows, dim), lambda i: (0, 0, i, 0, 0)),
        pl.BlockSpec((2, group, rows, dim), lambda i: (0, i, 0, 0)),
        pl.BlockSpec((slots - 1, 2, group, rows, dim), lambda i: (0, 0, i, 0, 0)),
        pl.BlockSpec((slots, 2, group, rows, dim), lambda i: (0, 0, i, 0, 0)),
    ]


def time_stats(side, qg, rb, ra, kv, group=8):
    slots, _, count, rows, dim = qg.shape
    half = slots * rows
    return pl.pallas_call(
        functools.partial(time_stats_kernel, scale=1.0 / math.sqrt(dim)),
        grid=(count // group,),
        in_specs=time_specs(group, slots, rows, dim),
        out_specs=pl.BlockSpec((2, group, 2 * half), lambda i: (0, i, 0)),
        out_shape=jax.ShapeDtypeStruct((2, count, 2 * half), F32),
        cost_estimate=pl.CostEstimate(
            flops=count * 2 * 2 * half * 2 * half * dim,
            bytes_accessed=qg.size * 2 * 3,
            transcendentals=count * half * 2 * half,
        ),
        compiler_params=pltpu.CompilerParams(vmem_limit_bytes=VMEM_LIMIT),
        name="time_stats",
    )(side, qg, rb, ra, kv)


def time_grads(side, qg, rb, ra, kv, mine, other, group=8):
    slots, _, count, rows, dim = qg.shape
    half = slots * rows
    stat = pl.BlockSpec((2, group, 2 * half), lambda i: (0, i, 0))
    return pl.pallas_call(
        functools.partial(time_grads_kernel, scale=1.0 / math.sqrt(dim)),
        grid=(count // group,),
        in_specs=time_specs(group, slots, rows, dim) + [stat, stat],
        out_specs=[
            pl.BlockSpec((slots, group, rows, dim), lambda i: (0, i, 0, 0)),
            pl.BlockSpec((group, rows, dim), lambda i: (i, 0, 0)),
            pl.BlockSpec((slots - 1, group, rows, dim), lambda i: (0, i, 0, 0)),
            pl.BlockSpec((slots, 2, group, rows, dim), lambda i: (0, 0, i, 0, 0)),
        ],
        out_shape=[
            jax.ShapeDtypeStruct((slots, count, rows, dim), F32),
            jax.ShapeDtypeStruct((count, rows, dim), BF16),
            jax.ShapeDtypeStruct((slots - 1, count, rows, dim), BF16),
            jax.ShapeDtypeStruct((slots, 2, count, rows, dim), BF16),
        ],
        cost_estimate=pl.CostEstimate(
            flops=count * 5 * 2 * half * 2 * half * dim,
            bytes_accessed=qg.size * 2 * 5,
            transcendentals=count * half * 2 * half,
        ),
        compiler_params=pltpu.CompilerParams(vmem_limit_bytes=VMEM_LIMIT),
        name="time_grads",
    )(side, qg, rb, ra, kv, mine, other)


def swap(x, bits):
    return lax.ppermute(x, "frame", [(i, i ^ bits) for i in range(FRAME_DEVICES)])


def from_side(x, side):
    pairs = [(i, i ^ ZHI_BIT) for i in range(FRAME_DEVICES) if (i // ZHI_BIT) % 2 == side]
    return lax.ppermute(x, "frame", pairs)


def pick(x, i):
    return lax.dynamic_index_in_dim(x, i, 0, keepdims=False)


def y_exchange(u, y):
    got = [swap(pick(u, y ^ j), j * Y_BIT) for j in range(1, 4)]
    for j in range(1, 4):
        u = lax.dynamic_update_index_in_dim(u, got[j - 1], y ^ j, 0)
    return u


def gather_frames(arrays, y, core):
    t = jnp.stack([jnp.transpose(a, (1, 2, 0, 3)) for a in arrays], 1)
    t = t.reshape((2, t.shape[0] // 2) + t.shape[1:])
    keep, got = pick(t, core), swap(pick(t, 1 - core), CORE_BIT)
    first = core == 0
    u = jnp.concatenate([jnp.where(first, keep, got), jnp.where(first, got, keep)], axis=-2)
    return y_exchange(u, y)


def scatter_frames(u, y, core):
    slots, n, count, rows, dim = u.shape
    t = jnp.transpose(u.reshape(slots, n, count, 2, rows // 2, dim), (0, 3, 1, 4, 2, 5))
    out = [jnp.zeros((rows // 2, 2 * slots, count, dim), u.dtype) for _ in range(n)]
    for j in range(slots):
        for c in range(2):
            piece = pick(pick(t, y ^ j), core ^ c)
            if j or c:
                piece = swap(piece, j * Y_BIT + c * CORE_BIT)
            head = (core ^ c) * slots + (y ^ j)
            out = [lax.dynamic_update_index_in_dim(o, piece[i], head, 1) for i, o in enumerate(out)]
    return out


def exchange_patches(x):
    return lax.all_to_all(x, "patch", split_axis=0, concat_axis=0, tiled=True)


def after(values, done):
    return lax.optimization_barrier(tuple(values) + (done,))


def per_device(q_space, k_space, v_space, d_out_space, q_time, k_time, v_time, d_out_time):
    frames, heads, rows, dim = q_space.shape
    seqs = frames * heads
    f = lax.axis_index("frame")
    y, side, core = f // Y_BIT, (f // ZHI_BIT) % 2, f % 2
    side_arr = jnp.reshape(side, (1,)).astype(jnp.int32)

    space = [a.reshape(seqs, rows, dim) for a in (q_space, k_space, v_space, d_out_space)]
    width = seqs // CHUNKS

    def space_part(c):
        x = stack_seqs(space, c * width, width)
        return x.reshape(PATCH_DEVICES, width // PATCH_DEVICES, 4, rows, dim)

    first, second = space_part(0), space_part(1)
    first = exchange_patches(first)
    qg = gather_frames((q_time, d_out_time), y, core)
    ra = swap(qg[1:], ZHI_BIT)
    rb = from_side(qg[0], 1)
    k_time, v_time, first, second, qg = after((k_time, v_time, first, second), qg)
    second = exchange_patches(second)
    kv = gather_frames((k_time, v_time), y, core)
    first = space_grads(first)

    kv, rb, first, second = lax.optimization_barrier((kv, rb, first, second))
    first, _ = after((first,), ra)
    first = exchange_patches(first)
    mine = time_stats(side_arr, qg, rb, ra, kv)
    other = swap(mine, ZHI_BIT)
    other = jnp.roll(other, other.shape[-1] // 2, axis=-1)
    second = space_grads(second)
    second, other = after((second,), other)
    dq, db, da, dkv = time_grads(side_arr, qg, rb, ra, kv, mine, other)
    db_sent, da_sent = from_side(db, 0), swap(da, ZHI_BIT)
    second, _ = after((second,), da)
    second = exchange_patches(second)
    dkv, first, db_sent = lax.optimization_barrier((dkv, first, db_sent))
    dk_time, dv_time = scatter_frames(dkv, y, core)
    dq, dk_time = after((dq,), dk_time)
    dq = (dq + jnp.concatenate([db_sent[None], da_sent]).astype(F32)).astype(BF16)
    (dq_time,) = scatter_frames(dq[:, None], y, core)
    second, dq_time = after((second,), dq_time)
    out = unstack_seqs(first.reshape(width, 3, rows, dim), 0, seqs)
    out = unstack_seqs(second.reshape(width, 3, rows, dim), width, seqs, out)
    out = [o.reshape(frames, heads, rows, dim) for o in out]
    return (out[0], out[1], out[2], dq_time, dk_time, dv_time)


def solution(mesh):
    spec = P("frame", None, "patch", None)
    return jax.shard_map(
        per_device, mesh=mesh, in_specs=(spec,) * 8, out_specs=(spec,) * 6, check_vma=False
    )
```

```python
import functools
import math

import jax
import jax.numpy as jnp
from jax import lax
from jax.experimental import pallas as pl
from jax.experimental.pallas import tpu as pltpu
from jax.sharding import PartitionSpec as P

F32 = jnp.float32
BF16 = jnp.bfloat16
LOG2E = 1.4426950408889634
MASKED = -1e30
VMEM_LIMIT = 40 * 1024 * 1024

CORE_BIT = 1
ZHI_BIT = 2
Y_BIT = 4
FRAME_DEVICES = 16
PATCH_DEVICES = 16
CHUNKS = 2


def dot(a, b, dims):
    return lax.dot_general(a, b, (dims, ((), ())), preferred_element_type=F32)


NT = ((1,), (1,))
NN = ((1,), (0,))
TN = ((0,), (0,))


def space_kernel(x_ref, o_ref, dk_acc, dv_acc, *, block, scale):
    peers, _, _, rows, dim = x_ref.shape
    length = peers * rows
    k = x_ref[:, 0, 1].reshape(length, dim)
    v = x_ref[:, 0, 2].reshape(length, dim)
    per = block // rows
    for b in range(length // block):
        q = x_ref[b * per : (b + 1) * per, 0, 0].reshape(block, dim)
        g = x_ref[b * per : (b + 1) * per, 0, 3].reshape(block, dim)
        s = dot(k, q, NT) * (scale * LOG2E)
        top = jnp.max(s, axis=0, keepdims=True)
        e = jnp.exp2(s - top)
        p = e * (1.0 / jnp.sum(e, axis=0, keepdims=True))
        w = p.astype(BF16)
        gv = dot(v, g, NT)
        delta = jnp.sum(p * gv, axis=0, keepdims=True)
        ds = (p * (gv - delta)).astype(BF16)
        dv = dot(w, g, NN)
        dk = dot(ds, q, NN)
        if b == 0:
            dv_acc[...] = dv
            dk_acc[...] = dk
        else:
            dv_acc[...] += dv
            dk_acc[...] += dk
        dq = dot(ds, k, TN) * scale
        o_ref[b * per : (b + 1) * per, 0, 0] = dq.astype(BF16).reshape(per, rows, dim)
    o_ref[:, 0, 1] = (dk_acc[...] * scale).astype(BF16).reshape(peers, rows, dim)
    o_ref[:, 0, 2] = dv_acc[...].astype(BF16).reshape(peers, rows, dim)


def space_grads(x):
    peers, seqs, _, rows, dim = x.shape
    length = peers * rows
    flops = seqs * 5 * 2 * length * length * dim
    return pl.pallas_call(
        functools.partial(space_kernel, block=256, scale=1.0 / math.sqrt(dim)),
        grid=(seqs,),
        in_specs=[pl.BlockSpec((peers, 1, 4, rows, dim), lambda j: (0, j, 0, 0, 0))],
        out_specs=pl.BlockSpec((peers, 1, 3, rows, dim), lambda j: (0, j, 0, 0, 0)),
        out_shape=jax.ShapeDtypeStruct((peers, seqs, 3, rows, dim), BF16),
        scratch_shapes=[pltpu.VMEM((length, dim), F32), pltpu.VMEM((length, dim), F32)],
        cost_estimate=pl.CostEstimate(
            flops=flops, bytes_accessed=x.size * 2 * 2, transcendentals=seqs * length * length
        ),
        compiler_params=pltpu.CompilerParams(vmem_limit_bytes=VMEM_LIMIT),
        name="space_grads",
    )(x)


def stack_kernel(q_ref, k_ref, v_ref, g_ref, o_ref):
    for i, x in enumerate((q_ref, k_ref, v_ref, g_ref)):
        o_ref[:, i] = x[...]


def stack_seqs(arrays, start, count, group=16):
    _, rows, dim = arrays[0].shape
    return pl.pallas_call(
        stack_kernel,
        grid=(count // group,),
        in_specs=[pl.BlockSpec((group, rows, dim), lambda i: (i + start // group, 0, 0))] * 4,
        out_specs=pl.BlockSpec((group, 4, rows, dim), lambda i: (i, 0, 0, 0)),
        out_shape=jax.ShapeDtypeStruct((count, 4, rows, dim), BF16),
        cost_estimate=pl.CostEstimate(flops=0, bytes_accessed=count * rows * dim * 16, transcendentals=0),
        name="stack_seqs",
    )(*arrays)


def unstack_kernel(x_ref, *refs):
    for i, o in enumerate(refs[-3:]):
        o[...] = x_ref[:, i]


def unstack_seqs(x, start, total, into=(), group=16):
    count, _, rows, dim = x.shape
    return pl.pallas_call(
        unstack_kernel,
        grid=(count // group,),
        in_specs=[pl.BlockSpec((group, 3, rows, dim), lambda i: (i, 0, 0, 0))]
        + [pl.BlockSpec(memory_space=pl.ANY)] * len(into),
        out_specs=[pl.BlockSpec((group, rows, dim), lambda i: (i + start // group, 0, 0))] * 3,
        out_shape=[jax.ShapeDtypeStruct((total, rows, dim), BF16)] * 3,
        input_output_aliases={i + 1: i for i in range(len(into))},
        cost_estimate=pl.CostEstimate(flops=0, bytes_accessed=count * rows * dim * 12, transcendentals=0),
        name="unstack_seqs",
    )(x, *into)


def time_rows(qg_ref, rb_ref, ra_ref, part, p):
    slots, _, _, rows, dim = qg_ref.shape
    half = slots * rows
    return jnp.concatenate(
        [
            qg_ref[:, part, p].reshape(half, dim),
            rb_ref[part, p],
            ra_ref[:, part, p].reshape(half - rows, dim),
        ]
    )


def time_allowed(side, slots, rows):
    half = slots * rows
    shape = (half, 2 * half)
    ki = lax.broadcasted_iota(jnp.int32, shape, 0)
    qi = lax.broadcasted_iota(jnp.int32, shape, 1)
    remote = qi // half
    qj = qi % half
    key_frame = (2 * (ki // rows) + side) * rows + ki % rows
    query_side = jnp.where(remote == 0, side, 1 - side)
    query_frame = (2 * (qj // rows) + query_side) * rows + qj % rows
    return key_frame <= query_frame


def time_stats_kernel(side_ref, qg_ref, rb_ref, ra_ref, kv_ref, st_ref, *, scale):
    slots, _, count, rows, _ = qg_ref.shape
    side = side_ref[0]
    half = slots * rows
    allowed = time_allowed(side, slots, rows)
    patches = range(count)
    dim = qg_ref.shape[-1]
    s = [dot(kv_ref[:, 0, p].reshape(half, dim), time_rows(qg_ref, rb_ref, ra_ref, 0, p), NT) for p in patches]
    gv = [dot(kv_ref[:, 1, p].reshape(half, dim), time_rows(qg_ref, rb_ref, ra_ref, 1, p), NT) for p in patches]
    s = [jnp.where(allowed, x * (scale * LOG2E), MASKED) for x in s]
    top = [jnp.max(x, axis=0, keepdims=True) for x in s]
    e = [jnp.exp2(x - t) for x, t in zip(s, top)]
    total = [jnp.sum(x, axis=0, keepdims=True) for x in e]
    part = [jnp.sum(x * y, axis=0, keepdims=True) for x, y in zip(e, gv)]
    st_ref[0] = jnp.concatenate([t + jnp.log2(x) for t, x in zip(top, total)])
    st_ref[1] = jnp.concatenate([x / y for x, y in zip(part, total)])


def time_totals(mine_ref, other_ref):
    lse_a, lse_b = mine_ref[0], other_ref[0]
    top = jnp.maximum(lse_a, lse_b)
    lse = top + jnp.log2(jnp.exp2(lse_a - top) + jnp.exp2(lse_b - top))
    delta = jnp.exp2(lse_a - lse) * mine_ref[1] + jnp.exp2(lse_b - lse) * other_ref[1]
    return lse, delta


def time_weights(allowed, s, gv, lse, delta):
    w = jnp.where(allowed, jnp.exp2(jnp.where(allowed, s - lse, 0.0)), 0.0)
    return w, (w * (gv - delta)).astype(BF16)


def time_grads_kernel(
    side_ref, qg_ref, rb_ref, ra_ref, kv_ref, mine_ref, other_ref, dq_ref, db_ref, da_ref, dkv_ref, *, scale
):
    slots, _, count, rows, dim = qg_ref.shape
    half = slots * rows
    allowed = time_allowed(side_ref[0], slots, rows)
    lse, delta = time_totals(mine_ref, other_ref)
    patches = range(count)
    k = [kv_ref[:, 0, p].reshape(half, dim) for p in patches]
    q = [time_rows(qg_ref, rb_ref, ra_ref, 0, p) for p in patches]
    g = [time_rows(qg_ref, rb_ref, ra_ref, 1, p) for p in patches]
    s = [dot(k[p], q[p], NT) * (scale * LOG2E) for p in patches]
    gv = [dot(kv_ref[:, 1, p].reshape(half, dim), g[p], NT) for p in patches]
    both = [time_weights(allowed, s[p], gv[p], lse[p : p + 1], delta[p : p + 1]) for p in patches]
    dv = [dot(both[p][0].astype(BF16), g[p], NN) for p in patches]
    dk = [dot(both[p][1], q[p], NN) for p in patches]
    dq = [dot(both[p][1], k[p], TN) for p in patches]
    for p in patches:
        dkv_ref[:, 1, p] = dv[p].astype(BF16).reshape(slots, rows, dim)
        dkv_ref[:, 0, p] = (dk[p] * scale).astype(BF16).reshape(slots, rows, dim)
        x = dq[p] * scale
        dq_ref[:, p] = x[:half].reshape(slots, rows, dim)
        db_ref[p] = x[half : half + rows].astype(BF16)
        da_ref[:, p] = x[half + rows :].astype(BF16).reshape(slots - 1, rows, dim)


def time_specs(group, slots, rows, dim):
    return [
        pl.BlockSpec(memory_space=pltpu.SMEM),
        pl.BlockSpec((slots, 2, group, rows, dim), lambda i: (0, 0, i, 0, 0)),
        pl.BlockSpec((2, group, rows, dim), lambda i: (0, i, 0, 0)),
        pl.BlockSpec((slots - 1, 2, group, rows, dim), lambda i: (0, 0, i, 0, 0)),
        pl.BlockSpec((slots, 2, group, rows, dim), lambda i: (0, 0, i, 0, 0)),
    ]


def time_stats(side, qg, rb, ra, kv, group=8):
    slots, _, count, rows, dim = qg.shape
    half = slots * rows
    return pl.pallas_call(
        functools.partial(time_stats_kernel, scale=1.0 / math.sqrt(dim)),
        grid=(count // group,),
        in_specs=time_specs(group, slots, rows, dim),
        out_specs=pl.BlockSpec((2, group, 2 * half), lambda i: (0, i, 0)),
        out_shape=jax.ShapeDtypeStruct((2, count, 2 * half), F32),
        cost_estimate=pl.CostEstimate(
            flops=count * 2 * 2 * half * 2 * half * dim,
            bytes_accessed=qg.size * 2 * 3,
            transcendentals=count * half * 2 * half,
        ),
        compiler_params=pltpu.CompilerParams(vmem_limit_bytes=VMEM_LIMIT),
        name="time_stats",
    )(side, qg, rb, ra, kv)


def time_grads(side, qg, rb, ra, kv, mine, other, group=8):
    slots, _, count, rows, dim = qg.shape
    half = slots * rows
    stat = pl.BlockSpec((2, group, 2 * half), lambda i: (0, i, 0))
    return pl.pallas_call(
        functools.partial(time_grads_kernel, scale=1.0 / math.sqrt(dim)),
        grid=(count // group,),
        in_specs=time_specs(group, slots, rows, dim) + [stat, stat],
        out_specs=[
            pl.BlockSpec((slots, group, rows, dim), lambda i: (0, i, 0, 0)),
            pl.BlockSpec((group, rows, dim), lambda i: (i, 0, 0)),
            pl.BlockSpec((slots - 1, group, rows, dim), lambda i: (0, i, 0, 0)),
            pl.BlockSpec((slots, 2, group, rows, dim), lambda i: (0, 0, i, 0, 0)),
        ],
        out_shape=[
            jax.ShapeDtypeStruct((slots, count, rows, dim), F32),
            jax.ShapeDtypeStruct((count, rows, dim), BF16),
            jax.ShapeDtypeStruct((slots - 1, count, rows, dim), BF16),
            jax.ShapeDtypeStruct((slots, 2, count, rows, dim), BF16),
        ],
        cost_estimate=pl.CostEstimate(
            flops=count * 5 * 2 * half * 2 * half * dim,
            bytes_accessed=qg.size * 2 * 5,
            transcendentals=count * half * 2 * half,
        ),
        compiler_params=pltpu.CompilerParams(vmem_limit_bytes=VMEM_LIMIT),
        name="time_grads",
    )(side, qg, rb, ra, kv, mine, other)


def swap(x, bits):
    return lax.ppermute(x, "frame", [(i, i ^ bits) for i in range(FRAME_DEVICES)])


def from_side(x, side):
    pairs = [(i, i ^ ZHI_BIT) for i in range(FRAME_DEVICES) if (i // ZHI_BIT) % 2 == side]
    return lax.ppermute(x, "frame", pairs)


def pick(x, i):
    return lax.dynamic_index_in_dim(x, i, 0, keepdims=False)


def y_exchange(u, y):
    got = [swap(pick(u, y ^ j), j * Y_BIT) for j in range(1, 4)]
    for j in range(1, 4):
        u = lax.dynamic_update_index_in_dim(u, got[j - 1], y ^ j, 0)
    return u


def gather_frames(arrays, y, core):
    t = jnp.stack([jnp.transpose(a, (1, 2, 0, 3)) for a in arrays], 1)
    t = t.reshape((2, t.shape[0] // 2) + t.shape[1:])
    keep, got = pick(t, core), swap(pick(t, 1 - core), CORE_BIT)
    first = core == 0
    u = jnp.concatenate([jnp.where(first, keep, got), jnp.where(first, got, keep)], axis=-2)
    return y_exchange(u, y)


def scatter_frames(u, y, core):
    slots, n, count, rows, dim = u.shape
    t = jnp.transpose(u.reshape(slots, n, count, 2, rows // 2, dim), (0, 3, 1, 4, 2, 5))
    out = [jnp.zeros((rows // 2, 2 * slots, count, dim), u.dtype) for _ in range(n)]
    for j, c in ((0, 0), (1, 0), (3, 0), (2, 0), (1, 1), (3, 1), (2, 1), (0, 1)):
        piece = pick(pick(t, y ^ j), core ^ c)
        if j or c:
            piece = swap(piece, j * Y_BIT + c * CORE_BIT)
        head = (core ^ c) * slots + (y ^ j)
        out = [lax.dynamic_update_index_in_dim(o, piece[i], head, 1) for i, o in enumerate(out)]
    return out


def exchange_patches(x):
    return lax.all_to_all(x, "patch", split_axis=0, concat_axis=0, tiled=True)


def after(values, done):
    return lax.optimization_barrier(tuple(values) + (done,))


def per_device(q_space, k_space, v_space, d_out_space, q_time, k_time, v_time, d_out_time):
    frames, heads, rows, dim = q_space.shape
    seqs = frames * heads
    f = lax.axis_index("frame")
    y, side, core = f // Y_BIT, (f // ZHI_BIT) % 2, f % 2
    side_arr = jnp.reshape(side, (1,)).astype(jnp.int32)

    space = [a.reshape(seqs, rows, dim) for a in (q_space, k_space, v_space, d_out_space)]
    width = seqs // CHUNKS

    def space_part(c):
        x = stack_seqs(space, c * width, width)
        return x.reshape(PATCH_DEVICES, width // PATCH_DEVICES, 4, rows, dim)

    first, second = space_part(0), space_part(1)
    first = exchange_patches(first)
    qg = gather_frames((q_time, d_out_time), y, core)
    ra = swap(qg[1:], ZHI_BIT)
    rb = from_side(qg[0], 1)
    k_time, v_time, first, second, qg = after((k_time, v_time, first, second), qg)
    second = exchange_patches(second)
    kv = gather_frames((k_time, v_time), y, core)
    first = space_grads(first)

    kv, rb, first, second = lax.optimization_barrier((kv, rb, first, second))
    first, _ = after((first,), ra)
    first = exchange_patches(first)
    mine = time_stats(side_arr, qg, rb, ra, kv)
    other = swap(mine, ZHI_BIT)
    other = jnp.roll(other, other.shape[-1] // 2, axis=-1)
    second = space_grads(second)
    second, other = after((second,), other)
    dq, db, da, dkv = time_grads(side_arr, qg, rb, ra, kv, mine, other)
    db_sent, da_sent = from_side(db, 0), swap(da, ZHI_BIT)
    second, _ = after((second,), da)
    second = exchange_patches(second)
    dkv, first = after((dkv,), first)
    dk_time, dv_time = scatter_frames(dkv, y, core)
    dq, dk_time = after((dq,), dk_time)
    dq = (dq + jnp.concatenate([db_sent[None], da_sent]).astype(F32)).astype(BF16)
    (dq_time,) = scatter_frames(dq[:, None], y, core)
    second, dq_time = after((second,), dq_time)
    out = unstack_seqs(first.reshape(width, 3, rows, dim), 0, seqs)
    out = unstack_seqs(second.reshape(width, 3, rows, dim), width, seqs, out)
    out = [o.reshape(frames, heads, rows, dim) for o in out]
    return (out[0], out[1], out[2], dq_time, dk_time, dv_time)


def solution(mesh):
    spec = P("frame", None, "patch", None)
    return jax.shard_map(
        per_device, mesh=mesh, in_specs=(spec,) * 8, out_specs=(spec,) * 6, check_vma=False
    )
```
